32 devices in a mesh: row: 4 (over y, core), col: 8 (over z, x).
Axes of the slice: x: 2, y: 2, z: 4, core: 2. Of those that a mesh axis runs over, the one named last changes fastest.
Arguments:
- slip: bfloat16 [32, 128, 3, 256], P(('row', 'col')), may hold values from -6 to 6
- near_pairs: int32 [512, 2], P(('row', 'col')), may hold values from 0 to 7, as said below
- near_blocks: bfloat16 [512, 768, 768], P(('row', 'col')), may hold values from -0.0546875 to 0.0546875
- near_live: int32 [32], P(('row', 'col')), may hold values from 1 to 16, as said below
- far_pairs: int32 [512, 2], P(('row', 'col')), may hold values from 0 to 7, as said below
- far_left: bfloat16 [512, 768, 32], P(('row', 'col')), may hold values from -0.21875 to 0.21875
- far_right: bfloat16 [512, 768, 32], P(('row', 'col')), may hold values from -0.21875 to 0.21875
Outputs:
- traction: bfloat16 [32, 128, 3, 256], P(('row', 'col'))
- response: bfloat16 [32, 128, 3, 256], P(('row', 'col'))
The draws below stay inside these ranges and needn't reach their ends.
Inputs may be any that keep to these rules, and one draw needn't show every extreme that they name: `near_pairs`: for a slot of group g, with a = g // 8, b = g % 8, first entry p and second entry q: p is below 8, q is below 4, and a * 8 + p <= q * 8 + b. `far_pairs`: the same rule as for the near-field pairs, with groups of 16 slots. `near_live`: some group has all 16 slots live.
All inputs are finite; a program needn't handle non-finite values.
Results may differ from the reference program's by a relative error of at most 0.022.
Values may be sent and summed in bfloat16 or wider, within the bound.
A program may use at most 192 MiB of HBM per device.

```python
import jax
import jax.numpy as jnp
from jax import lax

CL = 256
RANK = 32
NPD = 16
FPD = 16
SLIPS = 128
CLUSTERS = 32
NEAR_SLOTS = 512
FAR_SLOTS = 512
N_ROW = 4
N_COL = 8


def pair_draw(key, per_group):
    slots = N_ROW * N_COL * per_group
    group = jnp.arange(slots, dtype=jnp.int32) // per_group
    upper = group // N_COL
    across = group % N_COL
    first_key, second_key = jax.random.split(key)
    col_local = upper + jax.random.randint(first_key, (slots,), 0, 1 << 20, dtype=jnp.int32) % (N_ROW - upper)
    col_local = col_local.at[0].set(N_ROW - 1)
    limit = jnp.where(col_local > upper, N_COL, across + 1)
    row_local = jax.random.randint(second_key, (slots,), 0, 1 << 20, dtype=jnp.int32) % limit
    row_local = row_local.at[0].set(N_COL - 1)
    return jnp.stack([row_local, col_local], axis=1).astype(jnp.int32)


def draw_near_pairs(key, part):
    key = jax.random.fold_in(key, 11)
    return pair_draw(key, NPD)


def draw_far_pairs(key, part):
    key = jax.random.fold_in(key, 12)
    return pair_draw(key, FPD)


def draw_near_live(key, part):
    key = jax.random.fold_in(key, 13)
    first_key, second_key = jax.random.split(key)
    counts = jax.random.randint(first_key, (N_ROW * N_COL,), 1, NPD + 1, dtype=jnp.int32)
    fullest = jax.random.randint(second_key, (), 0, N_ROW * N_COL, dtype=jnp.int32)
    return counts.at[fullest].set(NPD).astype(jnp.int32)


def level_of(rng, extent, cuts, smallest, largest):
    factor_of, own = 1.0, jax.random.fold_in(rng, 6)
    for position, parts in cuts:
        heights = jnp.exp(jax.random.uniform(jax.random.fold_in(own, position), (parts,), jnp.float32, smallest / len(cuts), largest / len(cuts)))
        factor_of = factor_of * jnp.repeat(heights, extent[position] // parts).reshape([-1 if axis == position else 1 for axis in range(len(extent))])
    return factor_of


def scatter_about(key, extent, width, reach, shards=(), held_as=jnp.bfloat16):
    gain = level_of(key, extent, shards, -0.22, 0.18) if shards else 1.0
    values = jax.random.normal(key, extent, jnp.float32) * width * gain
    return jnp.minimum(jnp.maximum(values, -reach), reach).astype(held_as)


def setup_inputs(seed: int = 0) -> dict:
    key_list = jax.random.split(jax.random.key(seed), 8)
    slip = scatter_about(key_list[0], (CLUSTERS, SLIPS, 3, CL), 1.0, 6.0, ((0, 32),))
    near_pairs = draw_near_pairs(jax.random.fold_in(key_list[7], 71), 0)
    near_blocks = scatter_about(key_list[2], (NEAR_SLOTS, 3 * CL, 3 * CL), (3 * CL * NPD) ** -0.5, 0.0546875, ((0, 32),))
    near_live = draw_near_live(jax.random.fold_in(key_list[7], 71), 0)
    far_pairs = draw_far_pairs(jax.random.fold_in(key_list[7], 71), 0)
    far_left = scatter_about(key_list[5], (FAR_SLOTS, 3 * CL, RANK), (3 * CL) ** -0.5, 0.21875, ((0, 32),))
    far_right = scatter_about(key_list[6], (FAR_SLOTS, 3 * CL, RANK), (3 * CL) ** -0.5, 0.21875, ((0, 32),))
    return dict(slip=slip, near_pairs=near_pairs, near_blocks=near_blocks, near_live=near_live, far_pairs=far_pairs, far_left=far_left, far_right=far_right)


def one_product(slip_field, near_pairs, near_blocks, near_live, far_pairs, far_left, far_right):
    span_width = slip_field.shape[2] * slip_field.shape[3]
    slip_count = slip_field.shape[1]
    field = slip_field.reshape(slip_field.shape[0], slip_count, span_width).astype(jnp.float32)
    groups = near_live.shape[0]
    pair_list = near_pairs.reshape(groups, NPD, 2)
    block_list = near_blocks.reshape(groups, NPD, span_width, span_width)
    far_list = far_pairs.reshape(groups, FPD, 2)
    left_list = far_left.reshape(groups, FPD, span_width, RANK)
    right_list = far_right.reshape(groups, FPD, span_width, RANK)
    group_ids = jnp.arange(groups, dtype=jnp.int32)

    def device_step(totals, slot_items):
        pairs_here, blocks_here, live_count, far_here, left_factor, right_factor, group = slot_items
        upper = group // N_COL
        across = group % N_COL
        row_index = (upper * N_COL + pairs_here[:, 0]).astype(jnp.int32)
        col_index = (pairs_here[:, 1] * N_COL + across).astype(jnp.int32)
        live_mask = (jnp.arange(NPD, dtype=jnp.int32) < live_count).astype(jnp.float32)[:, None, None]
        blocks_wide = blocks_here.astype(jnp.float32)
        row_term = jnp.einsum('psb,pab->psa', field[col_index], blocks_wide) * live_mask
        col_term = jnp.einsum('psa,pab->psb', field[row_index], blocks_wide) * live_mask
        totals = totals.at[row_index].add(row_term).at[col_index].add(col_term)
        far_row = (upper * N_COL + far_here[:, 0]).astype(jnp.int32)
        far_col = (far_here[:, 1] * N_COL + across).astype(jnp.int32)
        left_wide = left_factor.astype(jnp.float32)
        right_wide = right_factor.astype(jnp.float32)
        coef_row = jnp.einsum('psw,pwk->psk', field[far_col], right_wide).astype(jnp.bfloat16)
        coef_row = lax.optimization_barrier(coef_row).astype(jnp.float32)
        coef_col = jnp.einsum('psw,pwk->psk', field[far_row], left_wide).astype(jnp.bfloat16)
        coef_col = lax.optimization_barrier(coef_col).astype(jnp.float32)
        totals = totals.at[far_row].add(jnp.einsum('psk,pwk->psw', coef_row, left_wide))
        totals = totals.at[far_col].add(jnp.einsum('psk,pwk->psw', coef_col, right_wide))
        return totals, None

    start = jnp.zeros(field.shape, jnp.float32)
    totals, _ = lax.scan(device_step, start, (pair_list, block_list, near_live, far_list, left_list, right_list, group_ids))
    return totals.astype(jnp.bfloat16).reshape(slip_field.shape)


def reference(slip, near_pairs, near_blocks, near_live, far_pairs, far_left, far_right):
    traction = one_product(slip, near_pairs, near_blocks, near_live, far_pairs, far_left, far_right)
    response = one_product(traction, near_pairs, near_blocks, near_live, far_pairs, far_left, far_right)
    return traction, response
```

```python
import functools

import jax
import jax.numpy as jnp
from jax import lax
from jax.experimental import pallas as pl
from jax.experimental.pallas import tpu as pltpu
from jax.sharding import PartitionSpec as P

MESH = pl.DeviceIdType.MESH
TRANS_B = (((1,), (1,)), ((), ()))


def both_products(dims, plan, field, planes, lcat, rcat, blocks_hbm, traction, response,
                  blocks, rg0, rg1, cg0, cg1, rp, xr, zr, zs, cp, cr, yr, ys, runs,
                  blk_sem, rg_rs, cg_rs, z_ss, x_ss, cgy_ss, cgc_ss,
                  xr_ss, xr_rs, zr_ss, zr_rs, cr_ss, cr_rs, yr_ss, yr_rs):
    A, B, R, S, parts = dims
    NC, NR = A * B, 2 * R
    slips, width = field.shape
    a, b = lax.axis_index("row"), lax.axis_index("col")
    z, x = b // B, b % B
    y, c = a // 2, a % 2
    f32, bf16 = jnp.float32, jnp.bfloat16

    def rcopy(src, dst, ss, rs, dev):
        return pltpu.make_async_remote_copy(
            src_ref=src, dst_ref=dst, send_sem=ss, recv_sem=rs, device_id=dev, device_id_type=MESH)

    part = S // parts
    for i in range(parts):
        pltpu.make_async_copy(blocks_hbm.at[pl.ds(i * part, part)], blocks.at[pl.ds(i * part, part)],
                              blk_sem.at[i]).start()
    for ref in (cg0, cg1):
        ref[...] = jnp.zeros(ref.shape, bf16)
    runs[0] = jnp.zeros((slips, width), f32)

    barrier = pltpu.get_barrier_semaphore()

    def hello(dev):
        pl.semaphore_signal(barrier, inc=1, device_id=dev, device_id_type=MESH)

    @pl.when(z > 0)
    def _():
        hello((a, b - B))

    @pl.when(z < A - 1)
    def _():
        hello((a, b + B))

    for j in range(1, B):
        hello((a, z * B + (x + j) % B))
    for j in range(1, R):
        hello((((y + j) % R) * 2 + c, b))
    hello((y * 2 + 1 - c, b))
    ends = jnp.where(z > 0, 1, 0) + jnp.where(z < A - 1, 1, 0)
    pl.semaphore_wait(barrier, ends + (B - 1) + (R - 1) + 1)

    def product(t, source, out):
        mine = source[...]
        rg, cg = ((rg0, cg0), (rg1, cg1))[t]
        rg[b] = mine
        cg[a] = mine
        partner = (y * 2 + 1 - c, b)

        def z_copy(zi, up, k):
            idx = zi * B + x
            return rcopy(rg.at[idx], rg.at[idx], z_ss.at[t, up, k], rg_rs.at[t, idx],
                         (a, b + B if up else b - B))

        def x_copy(zi, j, side, k):
            idx = zi * B + x
            return rcopy(rg.at[idx], rg.at[idx], x_ss.at[t, side, k, j - 1], rg_rs.at[t, idx],
                         (a, z * B + (x + j) % B))

        def z_cases(k):
            lo, hi = z - k, z + k
            return ((1, lo, lo >= 0, z < A - 1), (0, hi, hi < A, z > 0))

        def gather_step(k):
            for up, zi, valid, onward in z_cases(k):
                @pl.when(valid)
                def _(up=up, zi=zi, onward=onward):
                    if k > 0:
                        idx = zi * B + x
                        rcopy(rg.at[idx], rg.at[idx], z_ss.at[t, up, k], rg_rs.at[t, idx],
                              partner).wait_recv()
                    if k < A - 1:
                        @pl.when(onward)
                        def _():
                            z_copy(zi, up, k).start()
                    if k > 0 or up:
                        for j in range(1, B):
                            x_copy(zi, j, up, k).start()

        def gather_sent():
            for k in range(A):
                for up, zi, valid, onward in z_cases(k):
                    @pl.when(valid)
                    def _(up=up, zi=zi, onward=onward):
                        if k < A - 1:
                            @pl.when(onward)
                            def _():
                                z_copy(zi, up, k).wait_send()
                        if k > 0 or up:
                            for j in range(1, B):
                                x_copy(zi, j, up, k).wait_send()

        def y_copy(j):
            return rcopy(cg.at[a], cg.at[a], cgy_ss.at[t, j], cg_rs.at[t, a], (j * 2 + c, b))

        def c_copy(yi):
            idx = yi * 2 + c
            return rcopy(cg.at[idx], cg.at[idx], cgc_ss.at[t, yi], cg_rs.at[t, idx], partner)

        def cg_wait(idx):
            rcopy(cg.at[idx], cg.at[idx], cgc_ss.at[t, 0], cg_rs.at[t, idx], partner).wait_recv()

        gather_step(0)
        for j in range(R):
            @pl.when(j < y)
            def _(j=j):
                y_copy(j).start()
        for j in range(R):
            @pl.when(j == y)
            def _(j=j):
                c_copy(j).start()
        for j in range(R):
            @pl.when(j > y)
            def _(j=j):
                cg_wait(j * 2 + c)
                c_copy(j).start()
        if t == 0:
            for i in range(parts):
                pltpu.make_async_copy(blocks_hbm.at[pl.ds(i * part, part)],
                                      blocks.at[pl.ds(i * part, part)], blk_sem.at[i]).wait()
        gather_step(1)
        for j in range(R):
            @pl.when(j >= y)
            def _(j=j):
                cg_wait(j * 2 + 1 - c)

        def near(first, last, group, base, transposed):
            @pl.loop(first, last)
            def _(k):
                s = plan[base, k]
                keep = plan[base + 2, k].astype(f32)
                v = group[plan[base + 1, k]]
                if transposed:
                    term = lax.dot_general(v, blocks[s], TRANS_B, preferred_element_type=f32)
                else:
                    term = jnp.dot(v, blocks[s], preferred_element_type=f32)
                runs[k + 1] = runs[k] * keep + term

        def far(group, n, here, there, first, second, base, m, out_ref):
            w = first.shape[1]

            def gather_coef(i, coef):
                pair = group[pl.ds(2 * i, 2)].reshape(2 * slips, width)
                got = jnp.dot(pair, first[...], preferred_element_type=f32)
                coef = jnp.where(here == 2 * i, got[:slips], coef)
                return jnp.where(here == 2 * i + 1, got[slips:], coef)

            coef = lax.fori_loop(0, n // 2, gather_coef, jnp.zeros((slips, w), f32))

            @pl.loop(0, m // 2)
            def _(i):
                both = jnp.concatenate([jnp.where(there == 2 * i, coef, 0.0),
                                        jnp.where(there == 2 * i + 1, coef, 0.0)], axis=0).astype(bf16)
                terms = lax.dot_general(both, second[...], TRANS_B, preferred_element_type=f32)
                out_ref[t, 2 * i] = (terms[:slips] + runs[plan[base + 3, 2 * i]]).astype(bf16)
                out_ref[t, 2 * i + 1] = (terms[slips:] + runs[plan[base + 3, 2 * i + 1]]).astype(bf16)

        cuts = [S * i // (A - 1) for i in range(A)]
        for k in range(A - 1):
            near(cuts[k], cuts[k + 1], cg, 0, True)
            if k + 2 < A:
                gather_step(k + 2)
        row_lane = planes[0:1, :]
        col_lane = planes[1:2, :]
        far(cg, NR, col_lane, row_lane, rcat, lcat, 0, NC, rp)

        def xr_copy(zi, j):
            to = (x + j) % B
            return rcopy(rp.at[t, zi * B + to], xr.at[t, j - 1, zi], xr_ss.at[t, j - 1, zi],
                         xr_rs.at[t, j - 1, zi], (a, z * B + to))

        def targets(d):
            return ((1, z + d, z + d < A), (0, z - d, z - d >= 0))

        for d in range(A - 1, -1, -1):
            for up, zi, valid in targets(d):
                if d > 0 or up:
                    @pl.when(valid)
                    def _(zi=zi):
                        for j in range(1, B):
                            xr_copy(zi, j).start()

        for j in range(1, B):
            for zi in range(A):
                idx = zi * B + (x + j) % B
                rcopy(rg.at[idx], rg.at[idx], x_ss.at[t, 0, 0, 0], rg_rs.at[t, idx], partner).wait_recv()

        def zr_copy(zi, up):
            return rcopy(zs.at[t, zi], zr.at[t, up, zi], zr_ss.at[t, zi], zr_rs.at[t, up, zi],
                         (a, b + B if up else b - B))

        def x_sum(zi):
            total = rp[t, zi * B + x].astype(f32)
            for j in range(1, B):
                xr_copy(zi, j).wait_recv()
                total += xr[t, j - 1, zi].astype(f32)
            return total

        def reduce_step(d):
            for up, zi, valid in targets(d):
                @pl.when(valid)
                def _(up=up, zi=zi):
                    zs[t, zi] = x_sum(zi).astype(bf16)

                    @pl.when(z > 0 if up else z < A - 1)
                    def _():
                        zr_copy(zi, up).wait_recv()
                        zs[t, zi] = (zs[t, zi].astype(f32) + zr[t, up, zi].astype(f32)).astype(bf16)

                    zr_copy(zi, up).start()

        cuts = [S * i // A for i in range(A + 1)]
        near(cuts[0], cuts[1], rg, 4, False)
        for k in range(1, A):
            near(cuts[k], cuts[k + 1], rg, 4, False)
            if k > 1:
                reduce_step(A + 1 - k)
        far(rg, NC, row_lane, col_lane, lcat, rcat, 4, NR, cp)

        def cr_copy(yi):
            return rcopy(cp.at[t, yi * 2 + 1 - c], cr.at[t, yi], cr_ss.at[t, yi], cr_rs.at[t, yi], partner)

        def yr_copy(yi):
            return rcopy(ys.at[t, yi], yr.at[t, y], yr_ss.at[t, yi], yr_rs.at[t, y], (yi * 2 + c, b))

        for j in range(R):
            @pl.when(j >= y)
            def _(j=j):
                cr_copy(j).start()
        for j in range(R):
            @pl.when(j > y)
            def _(j=j):
                cr_copy(j).wait_recv()
                ys[t, j] = (cp[t, j * 2 + c].astype(f32) + cr[t, j].astype(f32)).astype(bf16)
                yr_copy(j).start()
        reduce_step(1)
        cr_copy(y).wait_recv()
        runs[1] = cp[t, y * 2 + c].astype(f32) + cr[t, y].astype(f32)
        for j in range(R):
            @pl.when(j < y)
            def _(j=j):
                rcopy(ys.at[t, j], yr.at[t, j], yr_ss.at[t, j], yr_rs.at[t, j], partner).wait_recv()
                runs[1] = runs[1] + yr[t, j].astype(f32)
        runs[1] = runs[1] + x_sum(z)
        for up in (1, 0):
            @pl.when(z > 0 if up else z < A - 1)
            def _(up=up):
                zr_copy(z, up).wait_recv()
                runs[1] = runs[1] + zr[t, up, z].astype(f32)
        out[...] = runs[1].astype(bf16)

        def sent():
            gather_sent()
            for j in range(R):
                @pl.when(j < y)
                def _(j=j):
                    y_copy(j).wait_send()

                @pl.when(j >= y)
                def _(j=j):
                    c_copy(j).wait_send()
                    cr_copy(j).wait_send()

                @pl.when(j > y)
                def _(j=j):
                    yr_copy(j).wait_send()
            for zi in range(A):
                for j in range(1, B):
                    xr_copy(zi, j).wait_send()

                @pl.when(zi != z)
                def _(zi=zi):
                    zr_copy(zi, 0).wait_send()

        return sent

    first_sent = product(0, field, traction)
    second_sent = product(1, traction, response)
    first_sent()
    second_sent()


def run_plan(own, other, live, slots, outs, width):
    key = jnp.where(jnp.arange(slots) < live, own, outs)
    ids = jnp.arange(slots, dtype=jnp.int32)
    before = (key[None, :] < key[:, None]) | ((key[None, :] == key[:, None]) & (ids[None, :] < ids[:, None]))
    rank = jnp.sum(before.astype(jnp.int32), axis=1)
    hot = (rank[None, :] == ids[:, None]).astype(jnp.int32)
    order = jnp.sum(hot * ids[None, :], axis=1)
    load = jnp.sum(hot * other[None, :], axis=1)
    same = (key[None, :] == key[:, None]) & (ids[None, :] != ids[:, None]) & (rank[None, :] < rank[:, None])
    keep = jnp.sum(hot * jnp.any(same, axis=1).astype(jnp.int32)[None, :], axis=1)
    marks = jnp.arange(width, dtype=jnp.int32)
    upto = jnp.sum((key[None, :] <= marks[:, None]).astype(jnp.int32), axis=1)
    has = jnp.any(key[None, :] == marks[:, None], axis=1) & (marks < outs)
    last = jnp.where(has, upto, 0)
    pad = lambda v: jnp.pad(v, (0, width - v.shape[0]))
    return [pad(order), pad(load), pad(keep), last]


def shards(slip, near_pairs, near_blocks, near_live, far_pairs, far_left, far_right):
    NR, NC = lax.axis_size("row"), lax.axis_size("col")
    A = 4 if NC % 4 == 0 else 2
    B, R = NC // A, NR // 2
    slips = slip.shape[1]
    width = slip.shape[2] * slip.shape[3]
    S = near_pairs.shape[0]
    FS, rank = far_pairs.shape[0], far_left.shape[2]
    parts = 4 if S % 4 == 0 else 1
    pw = max(S, NC, NR)
    p, q = near_pairs[:, 0], near_pairs[:, 1]
    plan = jnp.stack(run_plan(p, q, near_live[0], S, NC, pw) + run_plan(q, p, near_live[0], S, NR, pw))
    planes = jnp.repeat(far_pairs.T, rank, axis=1)
    lcat = far_left.transpose(1, 0, 2).reshape(width, FS * rank)
    rcat = far_right.transpose(1, 0, 2).reshape(width, FS * rank)
    field = slip.reshape(slips, width)
    bf16 = jnp.bfloat16
    buf = lambda *lead: pltpu.VMEM(lead + (slips, width), bf16)
    dma = lambda *shape: pltpu.SemaphoreType.DMA(shape)
    x_others = max(B - 1, 1)
    vmem = pl.BlockSpec(memory_space=pltpu.VMEM)
    traction, response = pl.pallas_call(
        functools.partial(both_products, (A, B, R, S, parts)),
        out_shape=(jax.ShapeDtypeStruct((slips, width), bf16),) * 2,
        in_specs=[pl.BlockSpec(memory_space=pltpu.SMEM), vmem, vmem, vmem, vmem,
                  pl.BlockSpec(memory_space=pl.ANY)],
        out_specs=(vmem, vmem),
        scratch_shapes=[
            pltpu.VMEM((S, width, width), bf16),
            buf(NC), buf(NC), buf(NR), buf(NR), buf(2, NC), buf(2, x_others, A), buf(2, 2, A), buf(2, A),
            buf(2, NR), buf(2, R), buf(2, R), buf(2, R),
            pltpu.VMEM((S + 1, slips, width), jnp.float32),
            dma(parts), dma(2, NC), dma(2, NR), dma(2, 2, A), dma(2, 2, A, x_others), dma(2, R), dma(2, R),
            dma(2, x_others, A), dma(2, x_others, A), dma(2, A), dma(2, 2, A),
            dma(2, R), dma(2, R), dma(2, R), dma(2, R),
        ],
        compiler_params=pltpu.CompilerParams(
            collective_id=0, has_side_effects=True, vmem_limit_bytes=60 * 1024 * 1024),
    )(plan, field, planes, lcat, rcat, near_blocks)
    return traction.reshape(slip.shape), response.reshape(slip.shape)


def solution(mesh):
    in_specs = (
        P(("row", "col"), None, None, None),
        P(("row", "col"), None),
        P(("row", "col"), None, None),
        P(("row", "col")),
        P(("row", "col"), None),
        P(("row", "col"), None, None),
        P(("row", "col"), None, None),
    )
    out_specs = (P(("row", "col"), None, None, None), P(("row", "col"), None, None, None))
    return jax.shard_map(shards, mesh=mesh, in_specs=in_specs, out_specs=out_specs, check_vma=False)
```

```python
import functools

import jax
import jax.numpy as jnp
from jax import lax
from jax.experimental import pallas as pl
from jax.experimental.pallas import tpu as pltpu
from jax.sharding import PartitionSpec as P

HALVES = 4
MESH = pl.DeviceIdType.MESH
TRANS_B = (((1,), (1,)), ((), ()))


def both_products(dims, plan, field, planes, lcat, rcat, blocks_hbm, traction, response,
                  blocks, rg0, rg1, cg0, cg1, rp, xr, zr, zs, cp, cr, yr, ys, runs,
                  blk_sem, rg_rs, cg_rs, z_ss, x_ss, cgy_ss, cgc_ss,
                  xr_ss, xr_rs, zr_ss, zr_rs, cr_ss, cr_rs, yr_ss, yr_rs):
    A, B, R, S, parts, H = dims
    NC, NR = A * B, 2 * R
    slips, width = field.shape
    a, b = lax.axis_index("row"), lax.axis_index("col")
    z, x = b // B, b % B
    y, c = a // 2, a % 2
    f32, bf16 = jnp.float32, jnp.bfloat16

    def rcopy(src, dst, ss, rs, dev):
        return pltpu.make_async_remote_copy(
            src_ref=src, dst_ref=dst, send_sem=ss, recv_sem=rs, device_id=dev, device_id_type=MESH)

    hr = slips // H

    def rows(h):
        return pl.ds(h * hr, hr)

    part = S // parts
    for i in range(parts):
        pltpu.make_async_copy(blocks_hbm.at[pl.ds(i * part, part)], blocks.at[pl.ds(i * part, part)],
                              blk_sem.at[i]).start()
    for ref in (cg0, cg1):
        ref[...] = jnp.zeros(ref.shape, bf16)
    runs[0] = jnp.zeros((slips, width), f32)

    barrier = pltpu.get_barrier_semaphore()

    def hello(dev):
        pl.semaphore_signal(barrier, inc=1, device_id=dev, device_id_type=MESH)

    @pl.when(z > 0)
    def _():
        hello((a, b - B))

    @pl.when(z < A - 1)
    def _():
        hello((a, b + B))

    for j in range(1, B):
        hello((a, z * B + (x + j) % B))
    for j in range(1, R):
        hello((((y + j) % R) * 2 + c, b))
    hello((y * 2 + 1 - c, b))
    ends = jnp.where(z > 0, 1, 0) + jnp.where(z < A - 1, 1, 0)
    pl.semaphore_wait(barrier, ends + (B - 1) + (R - 1) + 1)

    def product(t, source, out):
        mine = source[...]
        rg, cg = ((rg0, cg0), (rg1, cg1))[t]
        rg[b] = mine
        cg[a] = mine
        partner = (y * 2 + 1 - c, b)

        def z_copy(zi, up, k, h):
            idx = zi * B + x
            return rcopy(rg.at[idx, rows(h)], rg.at[idx, rows(h)], z_ss.at[t, up, k, h], rg_rs.at[t, idx, h],
                         (a, b + B if up else b - B))

        def x_copy(zi, j, side, k, h):
            idx = zi * B + x
            return rcopy(rg.at[idx, rows(h)], rg.at[idx, rows(h)], x_ss.at[t, side, k, h, j - 1],
                         rg_rs.at[t, idx, h], (a, z * B + (x + j) % B))

        def rg_wait(idx, h):
            rcopy(rg.at[idx, rows(h)], rg.at[idx, rows(h)], x_ss.at[t, 0, 0, h, 0], rg_rs.at[t, idx, h],
                  partner).wait_recv()

        def z_cases(k):
            lo, hi = z - k, z + k
            return ((1, lo, lo >= 0, z < A - 1), (0, hi, hi < A, z > 0))

        def gather_step(k, h):
            for up, zi, valid, onward in z_cases(k):
                @pl.when(valid)
                def _(up=up, zi=zi, onward=onward):
                    if k > 0:
                        rg_wait(zi * B + x, h)
                    if k < A - 1:
                        @pl.when(onward)
                        def _():
                            z_copy(zi, up, k, h).start()
                    if k > 0 or up:
                        for j in range(1, B):
                            x_copy(zi, j, up, k, h).start()

        def gather_sent():
            for k in range(A):
                for up, zi, valid, onward in z_cases(k):
                    @pl.when(valid)
                    def _(k=k, up=up, zi=zi, onward=onward):
                        for h in range(H):
                            if k < A - 1:
                                @pl.when(onward)
                                def _(h=h):
                                    z_copy(zi, up, k, h).wait_send()
                            if k > 0 or up:
                                for j in range(1, B):
                                    x_copy(zi, j, up, k, h).wait_send()

        def y_copy(j):
            return rcopy(cg.at[a], cg.at[a], cgy_ss.at[t, j], cg_rs.at[t, a], (j * 2 + c, b))

        def c_copy(yi):
            idx = yi * 2 + c
            return rcopy(cg.at[idx], cg.at[idx], cgc_ss.at[t, yi], cg_rs.at[t, idx], partner)

        def cg_wait(idx):
            rcopy(cg.at[idx], cg.at[idx], cgc_ss.at[t, 0], cg_rs.at[t, idx], partner).wait_recv()

        for h in range(H):
            gather_step(0, h)
        for j in range(R):
            @pl.when(j < y)
            def _(j=j):
                y_copy(j).start()
        for j in range(R):
            @pl.when(j == y)
            def _(j=j):
                c_copy(j).start()
        for j in range(R):
            @pl.when(j > y)
            def _(j=j):
                cg_wait(j * 2 + c)
                c_copy(j).start()
        if t == 0:
            for i in range(parts):
                pltpu.make_async_copy(blocks_hbm.at[pl.ds(i * part, part)],
                                      blocks.at[pl.ds(i * part, part)], blk_sem.at[i]).wait()
        for h in range(H):
            gather_step(1, h)
        for j in range(R):
            @pl.when(j >= y)
            def _(j=j):
                cg_wait(j * 2 + 1 - c)

        def near(first, last, group, base, transposed):
            @pl.loop(first, last)
            def _(k):
                s = plan[base, k]
                keep = plan[base + 2, k].astype(f32)
                v = group[plan[base + 1, k]]
                if transposed:
                    term = lax.dot_general(v, blocks[s], TRANS_B, preferred_element_type=f32)
                else:
                    term = jnp.dot(v, blocks[s], preferred_element_type=f32)
                runs[k + 1] = runs[k] * keep + term

        def far(group, n, here, there, first, second, base, m, out_ref):
            w = first.shape[1]

            def gather_coef(i, coef):
                pair = group[pl.ds(2 * i, 2)].reshape(2 * slips, width)
                got = jnp.dot(pair, first[...], preferred_element_type=f32)
                coef = jnp.where(here == 2 * i, got[:slips], coef)
                return jnp.where(here == 2 * i + 1, got[slips:], coef)

            coef = lax.fori_loop(0, n // 2, gather_coef, jnp.zeros((slips, w), f32))

            @pl.loop(0, m // 2)
            def _(i):
                both = jnp.concatenate([jnp.where(there == 2 * i, coef, 0.0),
                                        jnp.where(there == 2 * i + 1, coef, 0.0)], axis=0).astype(bf16)
                terms = lax.dot_general(both, second[...], TRANS_B, preferred_element_type=f32)
                out_ref[t, 2 * i] = (terms[:slips] + runs[plan[base + 3, 2 * i]]).astype(bf16)
                out_ref[t, 2 * i + 1] = (terms[slips:] + runs[plan[base + 3, 2 * i + 1]]).astype(bf16)

        steps = [(k, h) for k in range(2, A) for h in range(H)]
        n = len(steps) + 1
        cuts = [S * i // n for i in range(n + 1)]
        near(cuts[0], cuts[1], cg, 0, True)
        for i, (k, h) in enumerate(steps):
            gather_step(k, h)
            near(cuts[i + 1], cuts[i + 2], cg, 0, True)
        row_lane = planes[0:1, :]
        col_lane = planes[1:2, :]
        far(cg, NR, col_lane, row_lane, rcat, lcat, 0, NC, rp)

        def xr_copy(zi, j, h):
            to = (x + j) % B
            return rcopy(rp.at[t, zi * B + to, rows(h)], xr.at[t, j - 1, zi, rows(h)], xr_ss.at[t, j - 1, zi, h],
                         xr_rs.at[t, j - 1, zi, h], (a, z * B + to))

        def targets(d):
            return ((1, z + d, z + d < A), (0, z - d, z - d >= 0))

        for d in range(A - 1, -1, -1):
            for h in range(H):
                for up, zi, valid in targets(d):
                    if d > 0 or up:
                        @pl.when(valid)
                        def _(zi=zi, h=h):
                            for j in range(1, B):
                                xr_copy(zi, j, h).start()

        for j in range(1, B):
            for zi in range(A):
                for h in range(H):
                    rg_wait(zi * B + (x + j) % B, h)

        def zr_copy(zi, up, h):
            return rcopy(zs.at[t, zi, rows(h)], zr.at[t, up, zi, rows(h)], zr_ss.at[t, zi, h], zr_rs.at[t, up, zi, h],
                         (a, b + B if up else b - B))

        def x_sum(zi, h):
            total = rp[t, zi * B + x, rows(h)].astype(f32)
            for j in range(1, B):
                xr_copy(zi, j, h).wait_recv()
                total += xr[t, j - 1, zi, rows(h)].astype(f32)
            return total

        def reduce_step(d, h):
            for up, zi, valid in targets(d):
                @pl.when(valid)
                def _(up=up, zi=zi):
                    first = z == 0 if up else z == A - 1

                    @pl.when(first)
                    def _():
                        zs[t, zi, rows(h)] = x_sum(zi, h).astype(bf16)

                    @pl.when(jnp.logical_not(first))
                    def _():
                        total = x_sum(zi, h)
                        zr_copy(zi, up, h).wait_recv()
                        zs[t, zi, rows(h)] = (total + zr[t, up, zi, rows(h)].astype(f32)).astype(bf16)

                    zr_copy(zi, up, h).start()

        steps = [(d, h) for d in range(A - 1, 1, -1) for h in range(H)]
        n = len(steps) + 1
        cuts = [S * i // n for i in range(n + 1)]
        near(cuts[0], cuts[1], rg, 4, False)
        for i, (d, h) in enumerate(steps):
            reduce_step(d, h)
            near(cuts[i + 1], cuts[i + 2], rg, 4, False)
        far(rg, NC, row_lane, col_lane, lcat, rcat, 4, NR, cp)

        def cr_copy(yi):
            return rcopy(cp.at[t, yi * 2 + 1 - c], cr.at[t, yi], cr_ss.at[t, yi], cr_rs.at[t, yi], partner)

        def yr_copy(yi):
            return rcopy(ys.at[t, yi], yr.at[t, y], yr_ss.at[t, yi], yr_rs.at[t, y], (yi * 2 + c, b))

        for j in range(R):
            @pl.when(j >= y)
            def _(j=j):
                cr_copy(j).start()
        for j in range(R):
            @pl.when(j > y)
            def _(j=j):
                cr_copy(j).wait_recv()
                ys[t, j] = (cp[t, j * 2 + c].astype(f32) + cr[t, j].astype(f32)).astype(bf16)
                yr_copy(j).start()
        for h in range(H):
            reduce_step(1, h)
        cr_copy(y).wait_recv()
        runs[1] = cp[t, y * 2 + c].astype(f32) + cr[t, y].astype(f32)
        for j in range(R):
            @pl.when(j < y)
            def _(j=j):
                rcopy(ys.at[t, j], yr.at[t, j], yr_ss.at[t, j], yr_rs.at[t, j], partner).wait_recv()
                runs[1] = runs[1] + yr[t, j].astype(f32)
        for h in range(H):
            runs[1, rows(h)] = runs[1, rows(h)] + x_sum(z, h)
            for up in (1, 0):
                @pl.when(z > 0 if up else z < A - 1)
                def _(up=up, h=h):
                    zr_copy(z, up, h).wait_recv()
                    runs[1, rows(h)] = runs[1, rows(h)] + zr[t, up, z, rows(h)].astype(f32)
            out[rows(h)] = runs[1, rows(h)].astype(bf16)

        def sent():
            gather_sent()
            for j in range(R):
                @pl.when(j < y)
                def _(j=j):
                    y_copy(j).wait_send()

                @pl.when(j >= y)
                def _(j=j):
                    c_copy(j).wait_send()
                    cr_copy(j).wait_send()

                @pl.when(j > y)
                def _(j=j):
                    yr_copy(j).wait_send()
            for zi in range(A):
                for h in range(H):
                    for j in range(1, B):
                        xr_copy(zi, j, h).wait_send()

                    @pl.when(zi != z)
                    def _(zi=zi, h=h):
                        zr_copy(zi, 0, h).wait_send()

        return sent

    first_sent = product(0, field, traction)
    second_sent = product(1, traction, response)
    first_sent()
    second_sent()


def run_plan(own, other, live, slots, outs, width):
    key = jnp.where(jnp.arange(slots) < live, own, outs)
    ids = jnp.arange(slots, dtype=jnp.int32)
    before = (key[None, :] < key[:, None]) | ((key[None, :] == key[:, None]) & (ids[None, :] < ids[:, None]))
    rank = jnp.sum(before.astype(jnp.int32), axis=1)
    hot = (rank[None, :] == ids[:, None]).astype(jnp.int32)
    order = jnp.sum(hot * ids[None, :], axis=1)
    load = jnp.sum(hot * other[None, :], axis=1)
    same = (key[None, :] == key[:, None]) & (ids[None, :] != ids[:, None]) & (rank[None, :] < rank[:, None])
    keep = jnp.sum(hot * jnp.any(same, axis=1).astype(jnp.int32)[None, :], axis=1)
    marks = jnp.arange(width, dtype=jnp.int32)
    upto = jnp.sum((key[None, :] <= marks[:, None]).astype(jnp.int32), axis=1)
    has = jnp.any(key[None, :] == marks[:, None], axis=1) & (marks < outs)
    last = jnp.where(has, upto, 0)
    pad = lambda v: jnp.pad(v, (0, width - v.shape[0]))
    return [pad(order), pad(load), pad(keep), last]


def shards(slip, near_pairs, near_blocks, near_live, far_pairs, far_left, far_right):
    NR, NC = lax.axis_size("row"), lax.axis_size("col")
    A = 4 if NC % 4 == 0 else 2
    B, R = NC // A, NR // 2
    slips = slip.shape[1]
    width = slip.shape[2] * slip.shape[3]
    S = near_pairs.shape[0]
    FS, rank = far_pairs.shape[0], far_left.shape[2]
    parts = 4 if S % 4 == 0 else 1
    H = HALVES if slips % (16 * HALVES) == 0 else 1
    pw = max(S, NC, NR)
    p, q = near_pairs[:, 0], near_pairs[:, 1]
    plan = jnp.stack(run_plan(p, q, near_live[0], S, NC, pw) + run_plan(q, p, near_live[0], S, NR, pw))
    planes = jnp.repeat(far_pairs.T, rank, axis=1)
    lcat = far_left.transpose(1, 0, 2).reshape(width, FS * rank)
    rcat = far_right.transpose(1, 0, 2).reshape(width, FS * rank)
    field = slip.reshape(slips, width)
    bf16 = jnp.bfloat16
    buf = lambda *lead: pltpu.VMEM(lead + (slips, width), bf16)
    dma = lambda *shape: pltpu.SemaphoreType.DMA(shape)
    x_others = max(B - 1, 1)
    vmem = pl.BlockSpec(memory_space=pltpu.VMEM)
    traction, response = pl.pallas_call(
        functools.partial(both_products, (A, B, R, S, parts, H)),
        out_shape=(jax.ShapeDtypeStruct((slips, width), bf16),) * 2,
        in_specs=[pl.BlockSpec(memory_space=pltpu.SMEM), vmem, vmem, vmem, vmem,
                  pl.BlockSpec(memory_space=pl.ANY)],
        out_specs=(vmem, vmem),
        scratch_shapes=[
            pltpu.VMEM((S, width, width), bf16),
            buf(NC), buf(NC), buf(NR), buf(NR), buf(2, NC), buf(2, x_others, A), buf(2, 2, A), buf(2, A),
            buf(2, NR), buf(2, R), buf(2, R), buf(2, R),
            pltpu.VMEM((S + 1, slips, width), jnp.float32),
            dma(parts), dma(2, NC, H), dma(2, NR), dma(2, 2, A, H), dma(2, 2, A, H, x_others), dma(2, R), dma(2, R),
            dma(2, x_others, A, H), dma(2, x_others, A, H), dma(2, A, H), dma(2, 2, A, H),
            dma(2, R), dma(2, R), dma(2, R), dma(2, R),
        ],
        compiler_params=pltpu.CompilerParams(
            collective_id=0, has_side_effects=True, vmem_limit_bytes=60 * 1024 * 1024),
    )(plan, field, planes, lcat, rcat, near_blocks)
    return traction.reshape(slip.shape), response.reshape(slip.shape)


def solution(mesh):
    in_specs = (
        P(("row", "col"), None, None, None),
        P(("row", "col"), None),
        P(("row", "col"), None, None),
        P(("row", "col")),
        P(("row", "col"), None),
        P(("row", "col"), None, None),
        P(("row", "col"), None, None),
    )
    out_specs = (P(("row", "col"), None, None, None), P(("row", "col"), None, None, None))
    return jax.shard_map(shards, mesh=mesh, in_specs=in_specs, out_specs=out_specs, check_vma=False)
```
